32 devices in a mesh: blk: 8 (over z, core), tiles: 4 (over y, x).
Axes of the slice: x: 2, y: 2, z: 4, core: 2. Of those that a mesh axis runs over, the one named last changes fastest.
Arguments:
- tiles: bfloat16 [32, 128, 128, 128], P(('blk', 'tiles')), may hold values from -6 to 6
- live: int32 [32], P(('blk', 'tiles')), may hold values 0 or 1
- templates: bfloat16 [8, 64, 4096], P('blk', None, 'tiles'), may hold values from -0.01171875 to 0.01171875
Outputs:
- peak: float32 [32, 2, 128, 128], P(('blk', 'tiles'))
- mean_score: float32 [32, 2, 128, 128], P(('blk', 'tiles'))
The draws below stay inside these ranges and needn't reach their ends.
All inputs are finite; a program needn't handle non-finite values. No bound on the sum of `live` on one device may be relied on, other than what follows from the above.
Results may differ from the reference program's by a relative error of at most 0.0093.
Values may be sent and summed in bfloat16 or wider, within the bound.
A program may use at most 64 MiB of HBM per device.

```python
import math
import jax
import jax.numpy as jnp
from jax import lax

TX = 128
TY = 128
TZ = 128
TP = 64
OUTZ = 2
ROT = 8
TILES = 32


def plant(drawn, rng, smallest, high):
    spot = [jax.random.randint(jax.random.fold_in(rng, axis), (), 0, length) for axis, length in enumerate(drawn.shape)]
    widest = drawn.shape.index(max(drawn.shape))
    next_to = spot[:widest] + [(spot[widest] + 1) % drawn.shape[widest]] + spot[widest + 1:]
    return drawn.at[tuple(spot)].set(smallest).at[tuple(next_to)].set(high)


def levels(own_key, shape, shards, low, largest):
    level = 1.0
    for axis_at, blocks in shards:
        steps = jax.random.uniform(jax.random.fold_in(jax.random.fold_in(own_key, 6), axis_at), (blocks,), jnp.float32, low / len(shards), largest / len(shards))
        level = level * jnp.repeat(jnp.exp(steps), shape[axis_at] // blocks).reshape((-1,) + (1,) * (len(shape) - 1 - axis_at))
    return level


def bell_draw(stream_key, shape, scale, bound, shards=(), kind=jnp.bfloat16):
    values = scale * jax.random.normal(stream_key, shape, jnp.float32)
    if shards:
        values = values * levels(stream_key, shape, shards, -0.22, 0.18)
    return jnp.clip(values, -bound, bound).astype(kind)


def setup_inputs(seed: int = 0) -> dict:
    key_of = jax.random.split(jax.random.key(seed), 4)
    tiles = bell_draw(key_of[0], (TILES, TZ, TY, TX), 1.0, 6.0, ((0, 32),))
    live = plant((jax.random.randint(key_of[1], (TILES,), 0, 2) < 1).astype(jnp.int32), jax.random.fold_in(key_of[1], 1), 0, 1)
    templates = bell_draw(key_of[2], (ROT, TP, TP * TP), (TP * TP * TP) ** -0.5, 0.01171875, ((0, 8), (2, 4)))
    return {"tiles": tiles, "live": live, "templates": templates}


def tables(count, width):
    rows = jnp.arange(count, dtype=jnp.int32)[:, None]
    cols = jnp.arange(width, dtype=jnp.int32)[None, :]
    phase = ((rows * cols) % count).astype(jnp.float32) * (2.0 * math.pi / count)
    return jnp.cos(phase).astype(jnp.bfloat16), jnp.sin(phase).astype(jnp.bfloat16)


def mult(form, left, right):
    return jnp.einsum(form, left.astype(jnp.float32), right.astype(jnp.float32), precision=lax.Precision.HIGHEST)


def spectrum(volume, cosine_y, sine_y, cosine_x, sine_x):
    first_real = mult('...vu,kv->...ku', volume, cosine_y).astype(jnp.bfloat16)
    first_imag = (-mult('...vu,kv->...ku', volume, sine_y)).astype(jnp.bfloat16)
    out_real = (mult('...ku,hu->...kh', first_real, cosine_x) + mult('...ku,hu->...kh', first_imag, sine_x)).astype(jnp.bfloat16)
    out_imag = (mult('...ku,hu->...kh', first_imag, cosine_x) - mult('...ku,hu->...kh', first_real, sine_x)).astype(jnp.bfloat16)
    return out_real, out_imag


def correlate(pattern_real, pattern_imag, spectra_real, spectra_imag, cosine_x, sine_x, cosine_y, sine_y):
    edge = pattern_real.shape[0]
    plane_real = []
    plane_imag = []
    for offset in range(OUTZ):
        moved_real = jnp.roll(spectra_real, -offset, axis=-3)[..., :edge, :, :]
        moved_imag = jnp.roll(spectra_imag, -offset, axis=-3)[..., :edge, :, :]
        sum_real = mult('wkh,...wkh->...kh', pattern_real, moved_real) + mult('wkh,...wkh->...kh', pattern_imag, moved_imag)
        sum_imag = mult('wkh,...wkh->...kh', pattern_real, moved_imag) - mult('wkh,...wkh->...kh', pattern_imag, moved_real)
        plane_real.append(sum_real.astype(jnp.bfloat16))
        plane_imag.append(sum_imag.astype(jnp.bfloat16))
    prod_real = jnp.stack(plane_real, axis=-3)
    prod_imag = jnp.stack(plane_imag, axis=-3)
    back_real = (mult('...dkh,hx->...dkx', prod_real, cosine_x) - mult('...dkh,hx->...dkx', prod_imag, sine_x)).astype(jnp.bfloat16)
    back_imag = (mult('...dkh,hx->...dkx', prod_real, sine_x) + mult('...dkh,hx->...dkx', prod_imag, cosine_x)).astype(jnp.bfloat16)
    scale = 1.0 / (cosine_x.shape[0] * cosine_y.shape[0])
    return (mult('...dkx,ky->...dyx', back_real, cosine_y) - mult('...dkx,ky->...dyx', back_imag, sine_y)) * scale


def reference(tiles, live, templates):
    height = tiles.shape[2]
    width = tiles.shape[3]
    cosine_x, sine_x = tables(width, width)
    cosine_y, sine_y = tables(height, height)
    volumes = templates.reshape(ROT, TP, TP, TP)

    def template_spectrum(volume):
        return spectrum(volume, cosine_y[:, :TP], sine_y[:, :TP], cosine_x[:, :TP], sine_x[:, :TP])

    pattern_real, pattern_imag = lax.map(template_spectrum, volumes)

    def one_tile(inputs):
        tile, flag = inputs
        spectra_real, spectra_imag = spectrum(tile, cosine_y, sine_y, cosine_x, sine_x)

        def rotation_step(carry, pattern):
            scores = correlate(pattern[0], pattern[1], spectra_real, spectra_imag, cosine_x, sine_x, cosine_y, sine_y)
            return (jnp.maximum(carry[0], scores), carry[1] + scores), None

        start = (jnp.full((OUTZ, height, width), -jnp.inf, jnp.float32), jnp.zeros((OUTZ, height, width), jnp.float32))
        (highest, total), unused = lax.scan(rotation_step, start, (pattern_real, pattern_imag))
        factor = flag.astype(jnp.float32)
        return highest * factor, (total / ROT) * factor

    peak, mean_score = lax.map(one_tile, (tiles, live))
    return peak, mean_score
```

```python
import functools
import math

import jax
import jax.numpy as jnp
import numpy as np
from jax import lax
from jax.experimental import pallas as pl
from jax.experimental.pallas import tpu as pltpu
from jax.sharding import PartitionSpec as P

OUTZ = 2
MESH = pl.DeviceIdType.MESH
BF = jnp.bfloat16
F32 = jnp.float32


def tables(count, width):
    phase = (np.arange(count)[:, None] * np.arange(width)[None, :] % count).astype(np.float32)
    phase = phase * np.float32(2.0 * math.pi / count)
    return np.cos(phase).astype(np.float32), np.sin(phase).astype(np.float32)


def constants(height, width, edge, padded):
    half = height // 2 + 1
    cy, sy = tables(height, height)
    cx, sx = tables(width, width)
    rows = np.zeros((2 * padded, height), np.float32)
    rows[:half] = cy[:half]
    rows[padded : padded + half] = -sy[:half]
    tile_x = np.block([[cx.T, -sx.T], [sx.T, cx.T]])
    ce, se = cx[:, :edge].T, sx[:, :edge].T
    zero = np.zeros_like(ce)
    pair_x = np.block(
        [[ce, -se, zero, zero], [zero, zero, ce, -se], [se, ce, zero, zero], [zero, zero, se, ce]]
    )
    back_x = np.block([[cx, sx], [-sx, cx]])
    weight = np.full((half,), 2.0, np.float32)
    weight[0] = 1.0
    if height % 2 == 0:
        weight[-1] = 1.0
    weight = weight / (height * width)
    back_y = np.zeros((height, 2 * padded), np.float32)
    back_y[:, :half] = cy[:, :half].astype(jnp.bfloat16).astype(np.float32) * weight
    back_y[:, padded : padded + half] = -sy[:, :half].astype(jnp.bfloat16).astype(np.float32) * weight
    parts = (rows, rows[:, :edge], tile_x, pair_x, back_x, back_y)
    return tuple(jnp.asarray(np.ascontiguousarray(p).astype(jnp.bfloat16)) for p in parts)


def dot(left, right):
    return jnp.dot(left, right, preferred_element_type=F32)


def kernel(
    cfg, tile_hbm, own, tile_y, pat_y, tile_x, pair_x, back_x, back_y, peak, total,
    tile_buf, pieces, spectra, pattern, acc, tile_sem, send_sem, recv_sem,
):
    chips, count_t, padded, groups, edge, width = cfg
    bits = count_t.bit_length() - 1
    planes = tile_buf.shape[0]
    blk = lax.axis_index("blk")
    t = lax.axis_index("tiles")
    chip, core = blk // 2, blk % 2
    fetch = pltpu.make_async_copy(tile_hbm.at[0, pl.ds(0, planes)], tile_buf, tile_sem)
    fetch.start()

    def other(bit):
        size = 1 << bit
        return (blk, t + size - 2 * size * ((t // size) % 2))

    buddy = (blk + 1 - 2 * core, t)
    line = [(((chip + k) % chips) * 2 + core, t) for k in range(1, chips)]
    peers = line + [other(b) for b in range(bits)] + [buddy]
    barrier = pltpu.get_barrier_semaphore()
    for peer in peers:
        pl.semaphore_signal(barrier, inc=1, device_id=peer, device_id_type=MESH)
    pieces[0, 0, 0] = own[...]
    pl.semaphore_wait(barrier, len(peers))

    sends = []

    def send(src, dst, device):
        copy = pltpu.make_async_remote_copy(
            src_ref=pieces.at[src],
            dst_ref=pieces.at[dst],
            send_sem=send_sem.at[len(sends)],
            recv_sem=recv_sem.at[dst],
            device_id=device,
            device_id_type=MESH,
        )
        copy.start()
        sends.append(copy)

    def arrive(slot):
        pltpu.make_async_copy(pieces.at[slot], pieces.at[slot], recv_sem.at[slot]).wait()

    def service(k, stage):
        order = [(b + k) % bits for b in range(bits)]
        have = [0]
        for b in order[: max(stage - 1, 0)]:
            have = have + [h ^ (1 << b) for h in have]
        fresh = have
        if stage > 0:
            fresh = [h ^ (1 << order[stage - 1]) for h in have]
            have = have + fresh
        if stage > 0 or k > 0:
            for h in fresh:
                arrive((k, 0, h))
        if stage < bits:
            step = 1 << order[stage]
            for h in have:
                send((k, 0, h), (k, 0, h ^ step), other(order[stage]))
        for h in fresh:
            send((k, 0, h), (k, 1, h), buddy)

    for k in range(1, chips):
        send((0, 0, 0), (k, 0, 0), line[k - 1])
    service(0, 0)

    def tile_pairs(low, high):
        def body(p, carry):
            both = jnp.concatenate([tile_buf[2 * p], tile_buf[2 * p + 1]], axis=1)
            first = dot(tile_y[...], both).astype(BF)
            left = jnp.concatenate(
                [
                    jnp.concatenate(
                        [
                            first[:padded, j * width : (j + 1) * width],
                            first[padded:, j * width : (j + 1) * width],
                        ],
                        axis=1,
                    )
                    for j in range(2)
                ],
                axis=0,
            )
            out = dot(left, tile_x[...])
            spectra[2 * p] = out[:padded]
            spectra[2 * p + 1] = out[padded:]
            return carry

        lax.fori_loop(low, high, body, 0)

    def rotation(k, side, begin):
        acc[...] = jnp.zeros_like(acc)
        depth = 8
        lanes = depth * edge

        def body(q, carry):
            columns = pl.ds(pl.multiple_of(q * lanes, lanes), lanes)
            parts = []
            for source in range(count_t):
                slot = 0
                for b in range(bits):
                    size = 1 << b
                    slot = slot + size * (((source // size) + (t // size)) % 2)
                parts.append(pieces[k, side, slot, :, columns])
            first = dot(pat_y[...], jnp.concatenate(parts, axis=0)).astype(BF)
            left = jnp.concatenate(
                [
                    jnp.concatenate(
                        [
                            first[:padded, j * 2 * edge : (j + 1) * 2 * edge],
                            first[padded:, j * 2 * edge : (j + 1) * 2 * edge],
                        ],
                        axis=1,
                    )
                    for j in range(depth // 2)
                ],
                axis=0,
            )
            pattern[...] = dot(left, pair_x[...])
            for g in range(groups):
                rows = slice(8 * g, 8 * g + 8)
                sums = [acc[i, rows, :] for i in range(2 * OUTZ)]
                moved = [
                    (spectra[q * depth + d, rows, :width], spectra[q * depth + d, rows, width:])
                    for d in range(depth + OUTZ - 1)
                ]
                for w in range(depth):
                    at = (w // 2) * padded + 8 * g
                    shift = (w % 2) * 2 * width
                    a = pattern[at : at + 8, shift : shift + width]
                    b = pattern[at : at + 8, shift + width : shift + 2 * width]
                    for d in range(OUTZ):
                        c, e = moved[w + d]
                        sums[2 * d] = sums[2 * d] + (a * c + b * e)
                        sums[2 * d + 1] = sums[2 * d + 1] + (a * e - b * c)
                for i in range(2 * OUTZ):
                    acc[i, rows, :] = sums[i]
            return carry

        lax.fori_loop(0, edge // depth, body, 0)
        prod = jnp.concatenate(
            [
                jnp.concatenate([acc[2 * d].astype(BF), acc[2 * d + 1].astype(BF)], axis=1)
                for d in range(OUTZ)
            ],
            axis=0,
        )
        back = dot(prod, back_x[...]).astype(BF)
        right = jnp.concatenate(
            [
                jnp.concatenate(
                    [back[d * padded : (d + 1) * padded, i * width : (i + 1) * width] for d in range(OUTZ)],
                    axis=1,
                )
                for i in range(2)
            ],
            axis=0,
        )
        score = dot(back_y[...], right)
        for d in range(OUTZ):
            one = score[:, d * width : (d + 1) * width]
            if begin:
                peak[d] = one
                total[d] = one
            else:
                peak[d] = jnp.maximum(peak[d], one)
                total[d] = total[d] + one

    waiting = sorted(
        ((k, stage) for k in range(chips) for stage in range(bits + 1) if (k, stage) != (0, 0)),
        key=lambda item: (item[0] + item[1], item[0]),
    )

    def serve(level):
        while waiting and sum(waiting[0]) <= level:
            service(*waiting.pop(0))

    fetch.wait()
    pairs = planes // 2
    parts = bits + 1
    for i in range(parts):
        tile_pairs(pairs * i // parts, pairs * (i + 1) // parts)
        serve(i + 1)
    level = parts
    for k in range(chips):
        serve(k + bits)
        rotation(k, 0, k == 0)
        level += 1
        serve(level)
        for h in range(count_t):
            arrive((k, 1, h))
        rotation(k, 1, False)
        level += 1
        serve(level)
    for copy in sends:
        copy.wait_send()


def shards(tiles, live, templates):
    slots, depth, height, width = tiles.shape
    edge = templates.shape[1]
    nb, nt = lax.axis_size("blk"), lax.axis_size("tiles")
    count = templates.shape[0] * nb
    chips = nb // 2
    half = height // 2 + 1
    padded = -(-half // 16) * 16
    groups = -(-half // 8)
    planes = -(-(edge + OUTZ - 1) // 2) * 2
    piece_rows = templates.shape[2] // edge
    own = templates[0].reshape(edge, piece_rows, edge).transpose(1, 0, 2)
    own = own.reshape(piece_rows, edge * edge)
    mats = constants(height, width, edge, padded)
    bits = nt.bit_length() - 1
    n_sends = (chips - 1) + chips * ((nt - 1) + nt)
    vmem = pl.BlockSpec(memory_space=pltpu.VMEM)
    highest, total = pl.pallas_call(
        functools.partial(kernel, (chips, nt, padded, groups, edge, width)),
        out_shape=[jax.ShapeDtypeStruct((OUTZ, height, width), F32)] * 2,
        in_specs=[pl.BlockSpec(memory_space=pl.ANY)] + [vmem] * (1 + len(mats)),
        out_specs=[vmem, vmem],
        scratch_shapes=[
            pltpu.VMEM((planes, height, width), BF),
            pltpu.VMEM((chips, 2, nt, piece_rows, edge * edge), BF),
            pltpu.VMEM((planes, padded, 2 * width), F32),
            pltpu.VMEM((4 * padded, 4 * width), F32),
            pltpu.VMEM((2 * OUTZ, padded, width), F32),
            pltpu.SemaphoreType.DMA,
            pltpu.SemaphoreType.DMA((n_sends,)),
            pltpu.SemaphoreType.DMA((chips, 2, nt)),
        ],
        compiler_params=pltpu.CompilerParams(
            collective_id=0, has_side_effects=True, vmem_limit_bytes=48 * 1024 * 1024
        ),
    )(tiles, own, *mats)
    factor = (live > 0).astype(F32)[:, None, None, None]
    return (highest[None] * factor, total[None] / count * factor)


def solution(mesh):
    placed = (P(("blk", "tiles"), None, None, None), P(("blk", "tiles")), P("blk", None, "tiles"))
    return jax.shard_map(
        shards,
        mesh=mesh,
        in_specs=placed,
        out_specs=(P(("blk", "tiles"), None, None, None), P(("blk", "tiles"), None, None, None)),
        check_vma=False,
    )
```

```python
import functools
import math

import jax
import jax.numpy as jnp
import numpy as np
from jax import lax
from jax.experimental import pallas as pl
from jax.experimental.pallas import tpu as pltpu
from jax.sharding import PartitionSpec as P

OUTZ = 2
DEPTH = 32
TILE_STEP = 4
MESH = pl.DeviceIdType.MESH
BF = jnp.bfloat16
F32 = jnp.float32


def tables(count, width):
    phase = (np.arange(count)[:, None] * np.arange(width)[None, :] % count).astype(np.float32)
    phase = phase * np.float32(2.0 * math.pi / count)
    return np.cos(phase).astype(np.float32), np.sin(phase).astype(np.float32)


def constants(height, width, edge, padded):
    half = height // 2 + 1
    cy, sy = tables(height, height)
    cx, sx = tables(width, width)
    rows = np.zeros((2 * padded, height), np.float32)
    rows[:half] = cy[:half]
    rows[padded : padded + half] = -sy[:half]
    tile_x = np.block([[cx.T, -sx.T], [sx.T, cx.T]])
    ce, se = cx[:, :edge].T, sx[:, :edge].T
    zero = np.zeros_like(ce)
    pair_x = np.block(
        [[ce, -se, zero, zero], [zero, zero, ce, -se], [se, ce, zero, zero], [zero, zero, se, ce]]
    )
    back_x = np.block([[cx, sx], [-sx, cx]])
    weight = np.full((half,), 2.0, np.float32)
    weight[0] = 1.0
    if height % 2 == 0:
        weight[-1] = 1.0
    weight = weight / (height * width)
    back_y = np.zeros((height, 2 * padded), np.float32)
    back_y[:, :half] = cy[:, :half].astype(jnp.bfloat16).astype(np.float32) * weight
    back_y[:, padded : padded + half] = -sy[:, :half].astype(jnp.bfloat16).astype(np.float32) * weight
    parts = (rows, rows[:, :edge], tile_x, pair_x, back_x, back_y)
    places, top = [], 0
    for part in parts:
        places.append((top, part.shape[0], part.shape[1]))
        top += part.shape[0]
    whole = np.zeros((top, max(part.shape[1] for part in parts)), np.float32)
    for (start, high, wide), part in zip(places, parts):
        whole[start : start + high, :wide] = part
    return jnp.asarray(whole.astype(jnp.bfloat16)), places


def dot(left, right):
    return jnp.dot(left, right, preferred_element_type=F32)


def kernel(
    cfg, tile_hbm, mats_hbm, own, peak, total,
    tile_buf, mats, pieces, spectra, pattern, acc, prods, tile_sem, mats_sem, send_sem, recv_sem,
):
    chips, count_t, padded, groups, edge, width, places = cfg
    tile_y, pat_y, tile_x, pair_x, back_x, back_y = (
        mats.at[start : start + high, 0:wide] for start, high, wide in places
    )
    bits = count_t.bit_length() - 1
    planes = tile_buf.shape[0]
    blk = lax.axis_index("blk")
    t = lax.axis_index("tiles")
    chip, core = blk // 2, blk % 2
    fetch = pltpu.make_async_copy(tile_hbm.at[0, pl.ds(0, planes)], tile_buf, tile_sem)
    fetch.start()
    fetch_mats = pltpu.make_async_copy(mats_hbm, mats, mats_sem)
    fetch_mats.start()

    def other(bit):
        size = 1 << bit
        return (blk, t + size - 2 * size * ((t // size) % 2))

    buddy = (blk + 1 - 2 * core, t)
    line = [(((chip + k) % chips) * 2 + core, t) for k in range(1, chips)]
    peers = line + [other(b) for b in range(bits)] + [buddy]
    barrier = pltpu.get_barrier_semaphore()
    for peer in peers:
        pl.semaphore_signal(barrier, inc=1, device_id=peer, device_id_type=MESH)
    pieces[0, 0, 0] = own[...]
    pl.semaphore_wait(barrier, len(peers))

    sends = []

    def send(src, dst, device):
        copy = pltpu.make_async_remote_copy(
            src_ref=pieces.at[src],
            dst_ref=pieces.at[dst],
            send_sem=send_sem.at[len(sends)],
            recv_sem=recv_sem.at[dst],
            device_id=device,
            device_id_type=MESH,
        )
        copy.start()
        sends.append(copy)

    def arrive(slot):
        pltpu.make_async_copy(pieces.at[slot], pieces.at[slot], recv_sem.at[slot]).wait()

    def service(k, stage):
        order = [(b + k) % bits for b in range(bits)]
        have = [0]
        for b in order[: max(stage - 1, 0)]:
            have = have + [h ^ (1 << b) for h in have]
        fresh = have
        if stage > 0:
            fresh = [h ^ (1 << order[stage - 1]) for h in have]
            have = have + fresh
        if stage > 0 or k > 0:
            for h in fresh:
                arrive((k, 0, h))
        if stage < bits:
            step = 1 << order[stage]
            for h in have:
                send((k, 0, h), (k, 0, h ^ step), other(order[stage]))
        for h in fresh:
            send((k, 0, h), (k, 1, h), buddy)

    for k in range(1, chips):
        send((0, 0, 0), (k, 0, 0), line[k - 1])
    service(0, 0)

    pairs = planes // 2

    def tile_pairs(first_pair, count):
        for p in range(count):
            at = first_pair + p
            both = jnp.concatenate([tile_buf[2 * at], tile_buf[2 * at + 1]], axis=1)
            first = dot(tile_y[...], both).astype(BF)
            left = jnp.concatenate(
                [
                    jnp.concatenate(
                        [
                            first[:padded, j * width : (j + 1) * width],
                            first[padded:, j * width : (j + 1) * width],
                        ],
                        axis=1,
                    )
                    for j in range(2)
                ],
                axis=0,
            )
            out = dot(left, tile_x[...])
            spectra[2 * at] = out[:padded]
            spectra[2 * at + 1] = out[padded:]

    def tile_range(low, high):
        step = TILE_STEP

        def body(i, carry):
            tile_pairs(low + i * step, step)
            return carry

        lax.fori_loop(0, (high - low) // step, body, 0)
        if (high - low) % step:
            tile_pairs(high - (high - low) % step, (high - low) % step)

    def rotation(k, side, between):
        acc[...] = jnp.zeros_like(acc)
        depth = DEPTH
        lanes = depth * edge

        def body(q, carry):
            columns = pl.ds(pl.multiple_of(q * lanes, lanes), lanes)
            parts = []
            for source in range(count_t):
                slot = 0
                for b in range(bits):
                    size = 1 << b
                    slot = slot + size * (((source // size) + (t // size)) % 2)
                parts.append(pieces[k, side, slot, :, columns])
            first = dot(pat_y[...], jnp.concatenate(parts, axis=0)).astype(BF)
            left = jnp.concatenate(
                [
                    jnp.concatenate(
                        [
                            first[:padded, j * 2 * edge : (j + 1) * 2 * edge],
                            first[padded:, j * 2 * edge : (j + 1) * 2 * edge],
                        ],
                        axis=1,
                    )
                    for j in range(depth // 2)
                ],
                axis=0,
            )
            pattern[...] = dot(left, pair_x[...])
            for g in range(groups):
                rows = slice(8 * g, 8 * g + 8)
                sums = [acc[i, rows, :] for i in range(2 * OUTZ)]
                moved = [
                    (spectra[q * depth + d, rows, :width], spectra[q * depth + d, rows, width:])
                    for d in range(depth + OUTZ - 1)
                ]
                for w in range(depth):
                    at = (w // 2) * padded + 8 * g
                    shift = (w % 2) * 2 * width
                    a = pattern[at : at + 8, shift : shift + width]
                    b = pattern[at : at + 8, shift + width : shift + 2 * width]
                    for d in range(OUTZ):
                        c, e = moved[w + d]
                        sums[2 * d] = sums[2 * d] + (a * c + b * e)
                        sums[2 * d + 1] = sums[2 * d + 1] + (a * e - b * c)
                for i in range(2 * OUTZ):
                    acc[i, rows, :] = sums[i]
            return carry

        steps = edge // depth
        lax.fori_loop(0, steps // 2, body, 0)
        between()
        lax.fori_loop(steps // 2, steps, body, 0)
        base = (2 * k + side) * OUTZ * padded
        for d in range(OUTZ):
            for i in range(2):
                prods[base + d * padded : base + (d + 1) * padded, i * width : (i + 1) * width] = (
                    acc[2 * d + i].astype(BF)
                )

    def finish(group, count, begin):
        rows = count * OUTZ * padded
        back = dot(prods[group * rows : (group + 1) * rows], back_x[...]).astype(BF)
        best, added = [None] * OUTZ, [None] * OUTZ
        for r in range(count):
            base = r * OUTZ * padded
            right = jnp.concatenate(
                [
                    jnp.concatenate(
                        [
                            back[base + d * padded : base + (d + 1) * padded, i * width : (i + 1) * width]
                            for d in range(OUTZ)
                        ],
                        axis=1,
                    )
                    for i in range(2)
                ],
                axis=0,
            )
            score = dot(back_y[...], right)
            for d in range(OUTZ):
                one = score[:, d * width : (d + 1) * width]
                best[d] = one if r == 0 else jnp.maximum(best[d], one)
                added[d] = one if r == 0 else added[d] + one
        for d in range(OUTZ):
            if begin:
                peak[d] = best[d]
                total[d] = added[d]
            else:
                peak[d] = jnp.maximum(peak[d], best[d])
                total[d] = total[d] + added[d]

    order = [(0, stage) for stage in range(1, bits)] + [(k, 0) for k in range(1, chips)]
    order += [(k, stage) for stage in range(1, bits) for k in range(1, chips)]
    order.insert(bits + 1, (0, bits))
    order += [(k, bits) for k in range(1, chips)]
    waiting = list(order)

    def serve(steps=1):
        for _ in range(min(steps, len(waiting))):
            service(*waiting.pop(0))

    def need(item):
        while item in waiting:
            serve()

    fetch_mats.wait()
    fetch.wait()
    parts = bits + 1
    for i in range(parts):
        tile_range(pairs * i // parts, pairs * (i + 1) // parts)
        serve()
    for k in range(chips):
        need((k, bits))
        rotation(k, 0, serve)
        serve()
        for h in range(count_t):
            arrive((k, 1, h))
        rotation(k, 1, serve)
        serve()
        if k % 2 == 1:
            finish(k // 2, 4, k == 1)
    for copy in sends:
        copy.wait_send()


def shards(tiles, live, templates):
    slots, depth, height, width = tiles.shape
    edge = templates.shape[1]
    nb, nt = lax.axis_size("blk"), lax.axis_size("tiles")
    count = templates.shape[0] * nb
    chips = nb // 2
    half = height // 2 + 1
    padded = -(-half // 16) * 16
    groups = -(-half // 8)
    planes = -(-(edge + OUTZ - 1) // 2) * 2
    piece_rows = templates.shape[2] // edge
    own = templates[0].reshape(edge, piece_rows, edge).transpose(1, 0, 2)
    own = own.reshape(piece_rows, edge * edge)
    mats, places = constants(height, width, edge, padded)
    bits = nt.bit_length() - 1
    n_sends = (chips - 1) + chips * ((nt - 1) + nt)
    vmem = pl.BlockSpec(memory_space=pltpu.VMEM)
    highest, total = pl.pallas_call(
        functools.partial(kernel, (chips, nt, padded, groups, edge, width, places)),
        out_shape=[jax.ShapeDtypeStruct((OUTZ, height, width), F32)] * 2,
        in_specs=[pl.BlockSpec(memory_space=pl.ANY)] * 2 + [vmem],
        out_specs=[vmem, vmem],
        scratch_shapes=[
            pltpu.VMEM((planes, height, width), BF),
            pltpu.VMEM(mats.shape, BF),
            pltpu.VMEM((chips, 2, nt, piece_rows, edge * edge), BF),
            pltpu.VMEM((planes, padded, 2 * width), F32),
            pltpu.VMEM((DEPTH // 2 * padded, 4 * width), F32),
            pltpu.VMEM((2 * OUTZ, padded, width), F32),
            pltpu.VMEM((count * OUTZ * padded, 2 * width), BF),
            pltpu.SemaphoreType.DMA,
            pltpu.SemaphoreType.DMA,
            pltpu.SemaphoreType.DMA((n_sends,)),
            pltpu.SemaphoreType.DMA((chips, 2, nt)),
        ],
        compiler_params=pltpu.CompilerParams(
            collective_id=0, has_side_effects=True, vmem_limit_bytes=60 * 1024 * 1024
        ),
    )(tiles, mats, own)
    factor = (live > 0).astype(F32)[:, None, None, None]
    return (highest[None] * factor, total[None] / count * factor)


def solution(mesh):
    placed = (P(("blk", "tiles"), None, None, None), P(("blk", "tiles")), P("blk", None, "tiles"))
    return jax.shard_map(
        shards,
        mesh=mesh,
        in_specs=placed,
        out_specs=(P(("blk", "tiles"), None, None, None), P(("blk", "tiles"), None, None, None)),
        check_vma=False,
    )
```
